32 devices in a mesh: parts: 2 (over x), gx: 8 (over z, y), gy: 2 (over core).
Axes of the slice: x: 2, y: 2, z: 4, core: 2. Of those that a mesh axis runs over, the one named last changes fastest.
Arguments:
- features: bfloat16 [128, 512, 128], P(('parts', 'gx', 'gy')), parts along dimension 0, may hold values from -6 to 6
- cotangent: bfloat16 [128, 512, 128], P(('parts', 'gx', 'gy')), parts along dimension 0, may hold values from -6 to 6
- weights: bfloat16 [27, 128, 128], replicated, may hold values from -0.109375 to 0.109375
- neighbours: int32 [128, 27], P(('parts', 'gx', 'gy')), parts along dimension 0, may hold values from -1 to 63, as said below
- counts: int32 [32], P(('parts', 'gx', 'gy')), parts along dimension 0, may hold values from 2 to 4, as said below
Outputs:
- outputs: bfloat16 [128, 512, 128], P(('parts', 'gx', 'gy')), parts along dimension 0
- feature_grad: bfloat16 [128, 512, 128], P(('parts', 'gx', 'gy')), parts along dimension 0
- weight_grad: float32 [6912, 128], P('parts'), parts along dimension 0
The draws below stay inside these ranges and needn't reach their ends.
There are 2 independent parts, one for each index of `parts`. The reference program is written for one: setup_inputs(seed, part) draws one part's arguments, and reference() takes and returns one part's arrays. A program takes and returns all parts, laid end to end along the dimension named above; an argument that names none is the same for every part. Nothing has to cross between parts.
Inputs may be any that keep to these rules, and one draw needn't show every extreme that they name: `neighbours`: entries are -1 or the slot id of a live brick; the brick's device is at most one step away along gx and at most one along gy. The relation is symmetric, entry 13 of a live slot is the slot itself, and every row of a slot that is not live is all -1. `counts`: A device's live bricks are its first slots; some devices hold 4.
All inputs are finite; a program needn't handle non-finite values.
Results may differ from the reference program's by a relative error of at most 0.001.
Values may be sent and summed in bfloat16 or wider, within the bound.
A program may use at most 128 MiB of HBM per device.

```python
import jax
import jax.numpy as jnp
from jax import lax

C = 128
VOXELS = 512
BRICK_DEV = 4
NBRICK = 64
N_GY = 2


def layout(key):
    devices = NBRICK // BRICK_DEV
    count_key, place_key = jax.random.split(jax.random.fold_in(key, 11))
    tallies = jax.random.randint(count_key, (devices,), BRICK_DEV // 2, BRICK_DEV + 1)
    tallies = tallies.at[0].set(BRICK_DEV).at[devices - 1].set(BRICK_DEV).astype(jnp.int32)
    places = jax.vmap(lambda sub: jax.random.permutation(sub, 32))(jax.random.split(place_key, devices))[:, :BRICK_DEV]
    places = places.astype(jnp.int32)
    device_ids = jnp.arange(devices, dtype=jnp.int32)[:, None]
    coord_x = (device_ids // N_GY * 2 + places // 16).reshape(-1)
    coord_y = (device_ids % N_GY * 2 + places // 8 % 2).reshape(-1)
    coord_z = (places % 8).reshape(-1)
    alive = (jnp.arange(BRICK_DEV, dtype=jnp.int32)[None, :] < tallies[:, None]).reshape(-1)
    slot_ids = jnp.arange(NBRICK, dtype=jnp.int32)
    columns = []
    for step_x in range(3):
        for step_y in range(3):
            for step_z in range(3):
                match = coord_x[None, :] == coord_x[:, None] + step_x - 1
                match = match & (coord_y[None, :] == coord_y[:, None] + step_y - 1)
                match = match & (coord_z[None, :] == coord_z[:, None] + step_z - 1)
                match = match & alive[None, :] & alive[:, None]
                found = jnp.sum(jnp.where(match, slot_ids[None, :], 0), axis=1)
                columns.append(jnp.where(jnp.any(match, axis=1), found, -1))
    return (tallies, jnp.stack(columns, axis=1).astype(jnp.int32))


def draw_neighbours(key, part):
    tallies, table = layout(key)
    return table


def draw_counts(key, part):
    tallies, table = layout(key)
    return tallies


def block_levels(stream_key, extent, pieces, smallest, largest):
    level, own = 1.0, jax.random.fold_in(stream_key, 6)
    for dim, parts in pieces:
        draws = jnp.exp(jax.random.uniform(jax.random.fold_in(own, dim), (parts,), jnp.float32, smallest / len(pieces), largest / len(pieces)))
        level = level * jnp.repeat(draws, extent[dim] // parts).reshape([-1 if axis == dim else 1 for axis in range(len(extent))])
    return level


def noise(rng, extent, deviation, bound, cuts=(), held_as=jnp.bfloat16):
    loudness = block_levels(rng, extent, cuts, -0.22, 0.18) if cuts else 1.0
    values = jax.random.normal(rng, extent, jnp.float32) * deviation * loudness
    return jnp.minimum(jnp.maximum(values, -bound), bound).astype(held_as)


def setup_inputs(seed: int = 0, part: int = 0) -> dict:
    seeds = jax.random.split(jax.random.key(seed), 6)
    part_keys = jax.random.split(jax.random.fold_in(seeds[5], part), 6)
    return {
        "features": noise(part_keys[0], (NBRICK, VOXELS, C), 1.0, 6.0, ((0, 16),)),
        "cotangent": noise(part_keys[1], (NBRICK, VOXELS, C), 1.0, 6.0, ((0, 16),)),
        "weights": noise(seeds[2], (27, C, C), (27 * C) ** -0.5, 0.109375),
        "neighbours": draw_neighbours(jax.random.fold_in(jax.random.fold_in(seeds[5], part), 71), part),
        "counts": draw_counts(jax.random.fold_in(jax.random.fold_in(seeds[5], part), 71), part),
    }


def spans(step):
    if step == 0:
        return slice(7, 8), slice(0, 1)
    if step == 1:
        return slice(0, 8), slice(1, 9)
    return slice(0, 1), slice(9, 10)


def place(table, index):
    channels = table.shape[-1]
    cube = table.reshape(table.shape[0], 8, 8, 8, channels)
    slots = index.shape[0]
    padded = jnp.zeros((slots, 10, 10, 10, channels), table.dtype)
    for step_x in range(3):
        for step_y in range(3):
            for step_z in range(3):
                offset = step_x * 9 + step_y * 3 + step_z
                source_x, target_x = spans(step_x)
                source_y, target_y = spans(step_y)
                source_z, target_z = spans(step_z)
                picked = cube[index[:, offset]]
                padded = padded.at[:, target_x, target_y, target_z].set(picked[:, source_x, source_y, source_z])
    return padded


def reference(features, cotangent, weights, neighbours, counts):
    slots = features.shape[0]
    channels = features.shape[2]
    slot_ids = jnp.arange(slots, dtype=jnp.int32)
    owner_count = jnp.repeat(counts, BRICK_DEV)
    live = ((slot_ids % BRICK_DEV) < owner_count).astype(jnp.float32)[:, None, None]
    masked = (cotangent.astype(jnp.float32) * live).astype(cotangent.dtype)
    index = jnp.where(neighbours < 0, slots, neighbours).astype(jnp.int32)
    zero_row = jnp.zeros((1, VOXELS, channels), features.dtype)
    padded_x = place(jnp.concatenate([features, zero_row], axis=0), index)
    padded_g = place(jnp.concatenate([masked, zero_row], axis=0), index)
    rows = slots * VOXELS
    masked_rows = masked.reshape(rows, channels)
    out_acc = jnp.zeros((rows, channels), jnp.float32)
    grad_acc = jnp.zeros((rows, channels), jnp.float32)
    weight_terms = []
    for step_x in range(3):
        for step_y in range(3):
            for step_z in range(3):
                offset = step_x * 9 + step_y * 3 + step_z
                shifted = padded_x[:, step_x:step_x + 8, step_y:step_y + 8, step_z:step_z + 8].reshape(rows, channels)
                back = padded_g[:, 2 - step_x:10 - step_x, 2 - step_y:10 - step_y, 2 - step_z:10 - step_z].reshape(rows, channels)
                out_acc = out_acc + jnp.dot(shifted, weights[offset], preferred_element_type=jnp.float32)
                grad_acc = grad_acc + lax.dot_general(back, weights[offset], (((1,), (1,)), ((), ())), preferred_element_type=jnp.float32)
                weight_terms.append(lax.dot_general(shifted, masked_rows, (((0,), (0,)), ((), ())), preferred_element_type=jnp.float32))
    outputs = (out_acc.reshape(slots, VOXELS, channels) * live).astype(jnp.bfloat16)
    feature_grad = (grad_acc.reshape(slots, VOXELS, channels) * live).astype(jnp.bfloat16)
    weight_grad = jnp.stack(weight_terms, axis=0).reshape(27 * channels, channels)
    return outputs, feature_grad, weight_grad
```

```python
import functools

import jax
import jax.numpy as jnp
from jax import lax
from jax.experimental import pallas as pl
from jax.experimental.pallas import tpu as pltpu
from jax.sharding import PartitionSpec as P

MESH = pl.DeviceIdType.MESH
F32 = jnp.float32
BF16 = jnp.bfloat16


def kernel(
    n_gx,
    reduce_here,
    nb_ref,
    counts_ref,
    f_ref,
    g_ref,
    w_ref,
    out_ref,
    grad_ref,
    dw_ref,
    table_f,
    table_g,
    x_f,
    x_g,
    m_cat,
    w_back,
    acc,
    idx,
    part,
    got_core,
    got_y,
    got_z,
    own_sem,
    halo_send,
    halo_recv,
    red_send,
    red_recv,
):
    slots = f_ref.shape[0]
    tables = (table_f, table_g)
    nothing = 9 * slots
    rank = lax.axis_index("parts")
    gx = lax.axis_index("gx")
    gy = lax.axis_index("gy")
    other = 1 - gy
    up, down = lax.rem(gx + 1, n_gx), lax.rem(gx + n_gx - 1, n_gx)

    partners = [(up, gy), (down, gy), (gx, other), (up, other), (down, other)]
    if reduce_here:
        partners += [(lax.rem(gx + 2 * d, n_gx), gy) for d in (1, 2, 3)]
    barrier = pltpu.get_barrier_semaphore()
    for x, y in partners:
        pl.semaphore_signal(barrier, inc=1, device_id=(rank, x, y), device_id_type=MESH)

    own = [
        pltpu.make_async_copy(
            ref, tables[field].at[pl.ds(4 * slots, slots)], own_sem.at[field]
        )
        for field, ref in enumerate((f_ref, g_ref))
    ]
    for copy in own:
        copy.start()
    pl.semaphore_wait(barrier, len(partners))

    line = pl.ds(pl.multiple_of(48 * other, 16), 16)
    has_up, has_down = gx < n_gx - 1, gx > 0

    def halo(field, ref, kind):
        table = tables[field]
        if kind == 0:
            source = ref.at[:, 7]
            target = table.at[pl.ds(1 * slots, slots), 7]
            device = (rank, up, gy)
        elif kind == 1:
            source = ref.at[:, 0]
            target = table.at[pl.ds(7 * slots, slots), 0]
            device = (rank, down, gy)
        elif kind == 2:
            source = ref.at[:, :, line]
            target = table.at[pl.ds((3 + 2 * gy) * slots, slots), :, line]
            device = (rank, gx, other)
        elif kind == 3:
            source = ref.at[:, 7, line]
            target = table.at[pl.ds(2 * gy * slots, slots), 7, line]
            device = (rank, up, other)
        else:
            source = ref.at[:, 0, line]
            target = table.at[pl.ds((6 + 2 * gy) * slots, slots), 0, line]
            device = (rank, down, other)
        return pltpu.make_async_remote_copy(
            src_ref=source,
            dst_ref=target,
            send_sem=halo_send.at[field, kind],
            recv_sem=halo_recv.at[field, kind],
            device_id=device,
            device_id_type=MESH,
        )

    copies = [[halo(field, ref, kind) for kind in range(5)] for field, ref in enumerate((f_ref, g_ref))]

    def start(field):
        @pl.when(has_up)
        def _():
            copies[field][0].start()
            copies[field][3].start()

        @pl.when(has_down)
        def _():
            copies[field][1].start()
            copies[field][4].start()

        copies[field][2].start()

    def arrived(field):
        @pl.when(has_down)
        def _():
            copies[field][0].wait_recv()
            copies[field][3].wait_recv()

        @pl.when(has_up)
        def _():
            copies[field][1].wait_recv()
            copies[field][4].wait_recv()

        copies[field][2].wait_recv()

    def sent(field):
        @pl.when(has_up)
        def _():
            copies[field][0].wait_send()
            copies[field][3].wait_send()

        @pl.when(has_down)
        def _():
            copies[field][1].wait_send()
            copies[field][4].wait_send()

        copies[field][2].wait_send()

    start(0)
    start(1)

    def fill(n, carry):
        s, o = n // 27, n % 27
        entry = nb_ref[s, o]
        safe = jnp.maximum(entry, 0)
        owner = safe // slots
        relative = (owner // 2 - gx + 1) * 3 + (owner % 2 - gy + 1)
        place = jnp.where(entry < 0, nothing, relative * slots + safe % slots)
        idx[s, o] = jnp.minimum(jnp.maximum(place, 0), nothing)
        return carry

    lax.fori_loop(0, 27 * slots, fill, 0)

    for field in range(2):
        tables[field][nothing] = jnp.zeros(table_f.shape[1:], BF16)

    def turn(o, carry):
        rows = pl.ds(pl.multiple_of(o * 128, 128), 128)
        w_back[rows, :] = w_ref[26 - o].astype(F32).T.astype(BF16)
        return carry

    lax.fori_loop(0, 27, turn, 0)

    for copy in own:
        copy.wait()

    def spread(s, carry):
        base = pl.multiple_of(s * 640, 128)
        value = table_g[4 * slots + s].reshape(512, 128)
        value = jnp.where(s < counts_ref[0], value.astype(F32), 0.0).astype(BF16)
        for a in range(3):
            columns = slice(a * 128, a * 128 + 128)
            if a > 0:
                m_cat[pl.ds(base, a * 64), columns] = jnp.zeros((a * 64, 128), BF16)
            if a < 2:
                m_cat[pl.ds(base + a * 64 + 512, 128 - a * 64), columns] = jnp.zeros(
                    (128 - a * 64, 128), BF16
                )
            m_cat[pl.ds(base + a * 64, 512), columns] = value
        return carry

    lax.fori_loop(0, slots, spread, 0)

    sub = lax.broadcasted_iota(jnp.int32, (10, 8, 128), 1)

    def build(table, x_ref):
        def plane(n, carry):
            s, p = n // 10, n % 10
            first = jnp.where(p == 0, 0, jnp.where(p == 9, 18, 9))
            i = (p + 7) % 8

            def gathered(z):
                low = table[idx[s, first + z], i, 48:64].astype(F32)[8:]
                mid = table[idx[s, first + 3 + z], i].astype(F32)
                high = table[idx[s, first + 6 + z], i, 0:16].astype(F32)[:8]
                return jnp.concatenate([low, mid, high], axis=0).reshape(10, 8, 128)

            below, here, above = gathered(0), gathered(1), gathered(2)
            lower = pltpu.roll(jnp.where(sub == 7, below, here), 1, 1)
            upper = pltpu.roll(jnp.where(sub == 0, above, here), 7, 1)
            rows = pl.ds(pl.multiple_of(n * 64, 64), 64)
            for c, value in enumerate((lower, here, upper)):
                for b in range(3):
                    o = b * 3 + c
                    x_ref[rows, o * 128 : o * 128 + 128] = (
                        value[b : b + 8].reshape(64, 128).astype(BF16)
                    )
            return carry

        lax.fori_loop(0, 10 * slots, plane, 0)

    def product(x_ref, weight, result):
        def brick(s, carry):
            total = jnp.zeros((512, 128), F32)
            for a in range(3):
                rows = pl.ds(pl.multiple_of(s * 640 + a * 64, 64), 512)
                total += jnp.dot(
                    x_ref[rows, :],
                    weight[a * 1152 : a * 1152 + 1152, :],
                    preferred_element_type=F32,
                )
            result[s] = jnp.where(s < counts_ref[0], total, 0.0).astype(BF16)
            return carry

        lax.fori_loop(0, slots, brick, 0)

    def outer(t):
        acc[...] = jnp.zeros_like(acc)

        def brick(s, carry):
            rows = pl.ds(pl.multiple_of(s * 640, 128), 640)
            acc[...] += lax.dot_general(
                x_f[rows, t * 384 : t * 384 + 384],
                m_cat[rows, :],
                (((0,), (0,)), ((), ())),
                preferred_element_type=F32,
            )
            return carry

        lax.fori_loop(0, slots, brick, 0)
        target = part if reduce_here else dw_ref
        for a in range(3):
            for c in range(3):
                block = acc[c * 128 : c * 128 + 128, a * 128 : a * 128 + 128]
                target[a, t, c] = block.reshape(16, 8, 128)

    w_flat = w_ref.reshape(27 * 128, 128)

    arrived(0)
    build(table_f, x_f)
    if not reduce_here:
        for t in range(3):
            outer(t)
        arrived(1)
        build(table_g, x_g)
        product(x_f, w_flat, out_ref)
        product(x_g, w_back, grad_ref)
        sent(0)
        sent(1)
        return

    z, y = gx // 2, gx % 2
    half = 8 * gy
    quarter = half + 4 * y
    share = quarter + z
    side = (rank, z * 2 + 1 - y, gy)
    depth = [lax.rem(z + d, 4) for d in (1, 2, 3)]

    def send(t, k, source, target, device):
        return pltpu.make_async_remote_copy(
            src_ref=source,
            dst_ref=target,
            send_sem=red_send.at[t, k],
            recv_sem=red_recv.at[t, k],
            device_id=device,
            device_id_type=MESH,
        )

    core_step, y_step, z_step, z_back, y_back, core_back = [], [], [], [], [], []
    for t in range(3):
        core_step.append(
            send(t, 0, part.at[:, t, :, pl.ds(8 * other, 8)], got_core.at[t], (rank, gx, other))
        )
        y_step.append(
            send(t, 1, part.at[:, t, :, pl.ds(half + 4 * (1 - y), 4)], got_y.at[t], side)
        )
        z_step.append(
            [
                send(
                    t,
                    2 + d,
                    part.at[:, t, :, quarter + depth[d]],
                    got_z.at[t, d],
                    (rank, depth[d] * 2 + y, gy),
                )
                for d in range(3)
            ]
        )
        mine = dw_ref.at[:, t, :, share]
        z_back.append(
            [send(t, 5 + d, mine, mine, (rank, depth[d] * 2 + y, gy)) for d in range(3)]
        )
        mine = dw_ref.at[:, t, :, pl.ds(quarter, 4)]
        y_back.append(send(t, 8, mine, mine, side))
        mine = dw_ref.at[:, t, :, pl.ds(half, 8)]
        core_back.append(send(t, 9, mine, mine, (rank, gx, other)))

    def after_core(t):
        core_step[t].wait_recv()
        for a in range(3):
            for c in range(3):
                part[a, t, c, pl.ds(half, 8)] += got_core[t, a, c]
        y_step[t].start()

    def after_y(t):
        y_step[t].wait_recv()
        for a in range(3):
            for c in range(3):
                part[a, t, c, pl.ds(quarter, 4)] += got_y[t, a, c]
        for copy in z_step[t]:
            copy.start()

    def after_z(t):
        for copy in z_step[t]:
            copy.wait_recv()
        for a in range(3):
            for c in range(3):
                dw_ref[a, t, c, share] = (part[a, t, c, share] + got_z[t, 0, a, c]) + (
                    got_z[t, 1, a, c] + got_z[t, 2, a, c]
                )
        for copy in z_back[t]:
            copy.start()

    def after_z_back(t):
        for copy in z_back[t]:
            copy.wait_recv()
        y_back[t].start()

    def after_y_back(t):
        y_back[t].wait_recv()
        core_back[t].start()

    outer(0)
    core_step[0].start()
    outer(1)
    core_step[1].start()
    after_core(0)
    outer(2)
    core_step[2].start()
    after_core(1)
    arrived(1)
    build(table_g, x_g)
    after_core(2)
    after_y(0)
    product(x_f, w_flat, out_ref)
    after_y(1)
    after_z(0)
    after_y(2)
    product(x_g, w_back, grad_ref)
    after_z(1)
    after_z_back(0)
    after_z(2)
    after_z_back(1)
    after_y_back(0)
    after_z_back(2)
    after_y_back(1)
    after_y_back(2)
    for t in range(3):
        core_back[t].wait_recv()
    sent(0)
    sent(1)
    for t in range(3):
        for copy in [core_step[t], y_step[t], *z_step[t], *z_back[t], y_back[t], core_back[t]]:
            copy.wait_send()


def body(n_gx, features, cotangent, weights, neighbours, counts):
    slots, voxels, channels = features.shape
    reduce_here = n_gx == 8
    any_space = pl.BlockSpec(memory_space=pl.ANY)
    vmem = pl.BlockSpec(memory_space=pltpu.VMEM)
    smem = pl.BlockSpec(memory_space=pltpu.SMEM)
    rows = slots * 640
    outputs, grad, weight_grad = pl.pallas_call(
        functools.partial(kernel, n_gx, reduce_here),
        out_shape=(
            jax.ShapeDtypeStruct((slots, voxels, channels), BF16),
            jax.ShapeDtypeStruct((slots, voxels, channels), BF16),
            jax.ShapeDtypeStruct((3, 3, 3, 16, 8, channels), F32),
        ),
        in_specs=[smem, smem, any_space, any_space, vmem],
        out_specs=(vmem, vmem, vmem),
        scratch_shapes=[
            pltpu.VMEM((9 * slots + 1, 8, 64, channels), BF16),
            pltpu.VMEM((9 * slots + 1, 8, 64, channels), BF16),
            pltpu.VMEM((rows, 9 * channels), BF16),
            pltpu.VMEM((rows, 9 * channels), BF16),
            pltpu.VMEM((rows, 3 * channels), BF16),
            pltpu.VMEM((27 * channels, channels), BF16),
            pltpu.VMEM((3 * channels, 3 * channels), F32),
            pltpu.SMEM((slots, 27), jnp.int32),
            pltpu.VMEM((3, 3, 3, 16, 8, channels), F32),
            pltpu.VMEM((3, 3, 3, 8, 8, channels), F32),
            pltpu.VMEM((3, 3, 3, 4, 8, channels), F32),
            pltpu.VMEM((3, 3, 3, 3, 8, channels), F32),
            pltpu.SemaphoreType.DMA((2,)),
            pltpu.SemaphoreType.DMA((2, 5)),
            pltpu.SemaphoreType.DMA((2, 5)),
            pltpu.SemaphoreType.DMA((3, 10)),
            pltpu.SemaphoreType.DMA((3, 10)),
        ],
        compiler_params=pltpu.CompilerParams(
            collective_id=0, has_side_effects=True, vmem_limit_bytes=56 * 2**20
        ),
        cost_estimate=pl.CostEstimate(
            flops=6 * 27 * slots * voxels * channels * channels,
            bytes_accessed=8 * slots * voxels * channels,
            transcendentals=0,
        ),
    )(
        neighbours,
        counts,
        features.reshape(slots, 8, 64, channels),
        cotangent.reshape(slots, 8, 64, channels),
        weights,
    )
    weight_grad = weight_grad.reshape(27 * channels, channels)
    if not reduce_here:
        weight_grad = lax.psum(weight_grad, ("gx", "gy"))
    return outputs, grad, weight_grad


def solution(mesh):
    return jax.shard_map(
        functools.partial(body, mesh.shape["gx"]),
        mesh=mesh,
        in_specs=(
            P(("parts", "gx", "gy"), None, None),
            P(("parts", "gx", "gy"), None, None),
            P(),
            P(("parts", "gx", "gy"), None),
            P(("parts", "gx", "gy")),
        ),
        out_specs=(
            P(("parts", "gx", "gy"), None, None),
            P(("parts", "gx", "gy"), None, None),
            P("parts", None),
        ),
        check_vma=False,
    )
```

```python
import functools

import jax
import jax.numpy as jnp
from jax import lax
from jax.experimental import pallas as pl
from jax.experimental.pallas import tpu as pltpu
from jax.sharding import PartitionSpec as P

MESH = pl.DeviceIdType.MESH
F32 = jnp.float32
BF16 = jnp.bfloat16


def encode(values):
    largest = jnp.max(jnp.abs(values), axis=0, keepdims=True)
    exponent = jnp.floor(jnp.log2(jnp.maximum(largest, 1e-30)) + 0.01) - 14.0
    scaled = jnp.floor(values * jnp.exp2(-exponent) + 0.5)
    both = jnp.concatenate([scaled, exponent], axis=0)
    return both.astype(jnp.int32).reshape(80, 128).astype(jnp.int16)


def decode(coded):
    both = coded.astype(jnp.int32).astype(F32).reshape(10, 8, 128)
    return both[:9] * jnp.exp2(both[9:])


def finish(coded, q_ref, out_in, grad_in, out_ref, grad_ref, dw_ref, sem):
    copies = []
    for n in range(out_in.shape[0]):
        for k, (source, target) in enumerate(((out_in, out_ref), (grad_in, grad_ref))):
            copies.append(pltpu.make_async_copy(source.at[n], target.at[n], sem.at[k, n]))
    for copy in copies:
        copy.start()

    def piece(share, carry):
        for t in range(3):
            values = decode(q_ref[t, share]) if coded else q_ref[t, share]
            for a in range(3):
                for c in range(3):
                    dw_ref[a, t, c, share] = values[a * 3 + c]
        return carry

    lax.fori_loop(0, 16, piece, 0)
    for copy in copies:
        copy.wait()


def kernel(
    n_gx,
    reduce_here,
    nb_ref,
    counts_ref,
    f_ref,
    g_ref,
    w_hbm,
    out_hbm,
    grad_hbm,
    dw_ref,
    w_ref,
    out_ref,
    grad_ref,
    table_f,
    table_g,
    x_f,
    x_g,
    m_cat,
    w_back,
    acc,
    idx,
    part,
    got_core,
    y_out,
    got_y,
    z_out,
    got_z,
    own_sem,
    halo_send,
    halo_recv,
    red_send,
    red_recv,
):
    slots = f_ref.shape[0]
    tables = (table_f, table_g)
    nothing = 9 * slots
    bits = slots.bit_length() - 1
    assert slots == 1 << bits
    rank = lax.axis_index("parts")
    gx = lax.axis_index("gx")
    gy = lax.axis_index("gy")
    other = 1 - gy
    up, down = lax.rem(gx + 1, n_gx), lax.rem(gx + n_gx - 1, n_gx)

    partners = [(up, gy), (down, gy), (gx, other), (up, other), (down, other)]
    if reduce_here:
        partners += [(lax.rem(gx + 2 * d, n_gx), gy) for d in (1, 2, 3)]
    barrier = pltpu.get_barrier_semaphore()
    for x, y in partners:
        pl.semaphore_signal(barrier, inc=1, device_id=(rank, x, y), device_id_type=MESH)

    own = [
        pltpu.make_async_copy(
            ref, tables[field].at[pl.ds(4 * slots, slots)], own_sem.at[field]
        )
        for field, ref in enumerate((f_ref, g_ref))
    ]
    for copy in own:
        copy.start()
    weights_in = pltpu.make_async_copy(w_hbm, w_ref, own_sem.at[2])
    weights_in.start()
    out_copy = pltpu.make_async_copy(out_ref, out_hbm, own_sem.at[3])
    grad_copy = pltpu.make_async_copy(grad_ref, grad_hbm, own_sem.at[4])
    pl.semaphore_wait(barrier, len(partners))

    line = pl.ds(pl.multiple_of(48 * other, 16), 16)
    has_up, has_down = gx < n_gx - 1, gx > 0

    def halo(field, ref, kind):
        table = tables[field]
        if kind == 0:
            source = ref.at[:, 7]
            target = table.at[pl.ds(1 * slots, slots), 7]
            device = (rank, up, gy)
        elif kind == 1:
            source = ref.at[:, 0]
            target = table.at[pl.ds(7 * slots, slots), 0]
            device = (rank, down, gy)
        elif kind == 2:
            source = ref.at[:, :, line]
            target = table.at[pl.ds((3 + 2 * gy) * slots, slots), :, line]
            device = (rank, gx, other)
        elif kind == 3:
            source = ref.at[:, 7, line]
            target = table.at[pl.ds(2 * gy * slots, slots), 7, line]
            device = (rank, up, other)
        else:
            source = ref.at[:, 0, line]
            target = table.at[pl.ds((6 + 2 * gy) * slots, slots), 0, line]
            device = (rank, down, other)
        return pltpu.make_async_remote_copy(
            src_ref=source,
            dst_ref=target,
            send_sem=halo_send.at[field, kind],
            recv_sem=halo_recv.at[field, kind],
            device_id=device,
            device_id_type=MESH,
        )

    copies = [[halo(field, ref, kind) for kind in range(5)] for field, ref in enumerate((f_ref, g_ref))]

    def start(field):
        @pl.when(has_up)
        def _():
            copies[field][0].start()
            copies[field][3].start()

        @pl.when(has_down)
        def _():
            copies[field][1].start()
            copies[field][4].start()

        copies[field][2].start()

    def arrived(field):
        @pl.when(has_down)
        def _():
            copies[field][0].wait_recv()
            copies[field][3].wait_recv()

        @pl.when(has_up)
        def _():
            copies[field][1].wait_recv()
            copies[field][4].wait_recv()

        copies[field][2].wait_recv()

    def sent(field):
        @pl.when(has_up)
        def _():
            copies[field][0].wait_send()
            copies[field][3].wait_send()

        @pl.when(has_down)
        def _():
            copies[field][1].wait_send()
            copies[field][4].wait_send()

        copies[field][2].wait_send()

    start(0)

    def fill(s, carry):
        for o in range(27):
            entry = nb_ref[s, o]
            safe = jnp.maximum(entry, 0)
            owner = safe >> bits
            relative = ((owner >> 1) - gx + 1) * 3 + ((owner & 1) - gy + 1)
            place = jnp.where(entry < 0, nothing, relative * slots + (safe & (slots - 1)))
            idx[s, o] = jnp.minimum(jnp.maximum(place, 0), nothing)
        return carry

    lax.fori_loop(0, slots, fill, 0)

    for field in range(2):
        tables[field][nothing] = jnp.zeros(table_f.shape[1:], BF16)

    for copy in own:
        copy.wait()

    def spread(s, carry):
        base = pl.multiple_of(s * 640, 128)
        value = table_g[4 * slots + s].reshape(512, 128)
        value = jnp.where(s < counts_ref[0], value.astype(F32), 0.0).astype(BF16)
        for a in range(3):
            columns = slice(a * 128, a * 128 + 128)
            if a > 0:
                m_cat[pl.ds(base, a * 64), columns] = jnp.zeros((a * 64, 128), BF16)
            if a < 2:
                m_cat[pl.ds(base + a * 64 + 512, 128 - a * 64), columns] = jnp.zeros(
                    (128 - a * 64, 128), BF16
                )
            m_cat[pl.ds(base + a * 64, 512), columns] = value
        return carry

    lax.fori_loop(0, slots, spread, 0)

    def turn(o, carry):
        rows = pl.ds(pl.multiple_of(o * 128, 128), 128)
        w_back[rows, :] = w_ref[26 - o].astype(F32).T.astype(BF16)
        return carry

    sub = lax.broadcasted_iota(jnp.int32, (10, 8, 128), 1)

    def build(table, x_ref):
        def plane(s, p, first, i):
            def gathered(z):
                low = table[idx[s, first + z], i, 48:64].astype(F32)[8:]
                mid = table[idx[s, first + 3 + z], i].astype(F32)
                high = table[idx[s, first + 6 + z], i, 0:16].astype(F32)[:8]
                return jnp.concatenate([low, mid, high], axis=0).reshape(10, 8, 128)

            below, here, above = gathered(0), gathered(1), gathered(2)
            lower = pltpu.roll(jnp.where(sub == 7, below, here), 1, 1)
            upper = pltpu.roll(jnp.where(sub == 0, above, here), 7, 1)
            rows = pl.ds(pl.multiple_of(s * 640 + p * 64, 64), 64)
            for c, value in enumerate((lower, here, upper)):
                for b in range(3):
                    o = b * 3 + c
                    x_ref[rows, o * 128 : o * 128 + 128] = (
                        value[b : b + 8].reshape(64, 128).astype(BF16)
                    )

        def brick(s, carry):
            plane(s, 0, 0, 7)
            plane(s, 9, 18, 0)

            def inner(i, carry):
                plane(s, i + 1, 9, i)
                return carry

            return lax.fori_loop(0, 8, inner, carry)

        lax.fori_loop(0, slots, brick, 0)

    def product(x_ref, weight, result):
        def brick(s, carry):
            total = jnp.zeros((512, 128), F32)
            for a in range(3):
                rows = pl.ds(pl.multiple_of(s * 640 + a * 64, 64), 512)
                total += jnp.dot(
                    x_ref[rows, :],
                    weight[a * 1152 : a * 1152 + 1152, :],
                    preferred_element_type=F32,
                )
            result[s] = jnp.where(s < counts_ref[0], total, 0.0).astype(BF16)
            return carry

        lax.fori_loop(0, slots, brick, 0)

    def outer(t):
        acc[...] = jnp.zeros_like(acc)

        def brick(s, carry):
            rows = pl.ds(pl.multiple_of(s * 640, 128), 640)
            acc[...] += lax.dot_general(
                x_f[rows, t * 384 : t * 384 + 384],
                m_cat[rows, :],
                (((0,), (0,)), ((), ())),
                preferred_element_type=F32,
            )
            return carry

        lax.fori_loop(0, slots, brick, 0)
        target = part if reduce_here else dw_ref
        for a in range(3):
            for c in range(3):
                block = acc[c * 128 : c * 128 + 128, a * 128 : a * 128 + 128]
                target[t, :, a * 3 + c] = block.reshape(16, 8, 128)

    w_flat = w_ref.reshape(27 * 128, 128)

    arrived(0)
    start(1)
    build(table_f, x_f)
    if not reduce_here:
        for t in range(3):
            outer(t)
        arrived(1)
        build(table_g, x_g)
        weights_in.wait()
        product(x_f, w_flat, out_ref)
        out_copy.start()
        lax.fori_loop(0, 27, turn, 0)
        product(x_g, w_back, grad_ref)
        grad_copy.start()
        out_copy.wait()
        grad_copy.wait()
        sent(0)
        sent(1)
        return

    z, y = gx // 2, gx % 2
    half = 8 * gy
    quarter = half + 4 * y
    share = quarter + z
    side = (rank, z * 2 + 1 - y, gy)
    depth = [lax.rem(z + d, 4) for d in (1, 2, 3)]

    def send(t, k, source, target, device):
        return pltpu.make_async_remote_copy(
            src_ref=source,
            dst_ref=target,
            send_sem=red_send.at[t, k],
            recv_sem=red_recv.at[t, k],
            device_id=device,
            device_id_type=MESH,
        )

    core_step, y_step, z_step, z_back, y_back, core_back = [], [], [], [], [], []
    for t in range(3):
        core_step.append(
            send(t, 0, part.at[t, pl.ds(8 * other, 8)], got_core.at[t], (rank, gx, other))
        )
        y_step.append(send(t, 1, y_out.at[t], got_y.at[t], side))
        z_step.append(
            [
                send(t, 2 + d, z_out.at[t, d], got_z.at[t, d], (rank, depth[d] * 2 + y, gy))
                for d in range(3)
            ]
        )
        mine = dw_ref.at[t, share]
        z_back.append(
            [send(t, 5 + d, mine, mine, (rank, depth[d] * 2 + y, gy)) for d in range(3)]
        )
        mine = dw_ref.at[t, pl.ds(quarter, 4)]
        y_back.append(send(t, 8, mine, mine, side))
        mine = dw_ref.at[t, pl.ds(half, 8)]
        core_back.append(send(t, 9, mine, mine, (rank, gx, other)))

    def after_core(t):
        core_step[t].wait_recv()
        for j in range(4):
            place = 4 * (1 - y) + j
            y_out[t, j] = encode(part[t, half + place] + got_core[t, place])
        y_step[t].start()
        for j in range(4):
            place = 4 * y + j
            part[t, half + place] += got_core[t, place]

    def after_y(t):
        y_step[t].wait_recv()
        for d in range(3):
            z_out[t, d] = encode(part[t, quarter + depth[d]] + decode(got_y[t, depth[d]]))
        for copy in z_step[t]:
            copy.start()
        part[t, share] += decode(got_y[t, z])

    def after_z(t):
        for copy in z_step[t]:
            copy.wait_recv()
        dw_ref[t, share] = encode(
            (part[t, share] + decode(got_z[t, 0]))
            + (decode(got_z[t, 1]) + decode(got_z[t, 2]))
        )
        for copy in z_back[t]:
            copy.start()

    def after_z_back(t):
        for copy in z_back[t]:
            copy.wait_recv()
        y_back[t].start()

    def after_y_back(t):
        y_back[t].wait_recv()
        core_back[t].start()

    outer(0)
    core_step[0].start()
    outer(1)
    core_step[1].start()
    after_core(0)
    outer(2)
    core_step[2].start()
    after_core(1)
    arrived(1)
    after_core(2)
    build(table_g, x_g)
    after_y(0)
    weights_in.wait()
    product(x_f, w_flat, out_ref)
    out_copy.start()
    after_y(1)
    after_z(0)
    after_y(2)
    lax.fori_loop(0, 27, turn, 0)
    product(x_g, w_back, grad_ref)
    grad_copy.start()
    after_z(1)
    after_z_back(0)
    after_z(2)
    after_z_back(1)
    after_y_back(0)
    after_z_back(2)
    after_y_back(1)
    after_y_back(2)
    for t in range(3):
        core_back[t].wait_recv()
    out_copy.wait()
    grad_copy.wait()
    sent(0)
    sent(1)
    for t in range(3):
        for copy in [core_step[t], y_step[t], *z_step[t], *z_back[t], y_back[t], core_back[t]]:
            copy.wait_send()


def body(n_gx, features, cotangent, weights, neighbours, counts):
    slots, voxels, channels = features.shape
    reduce_here = n_gx == 8
    any_space = pl.BlockSpec(memory_space=pl.ANY)
    vmem = pl.BlockSpec(memory_space=pltpu.VMEM)
    smem = pl.BlockSpec(memory_space=pltpu.SMEM)
    rows = slots * 640
    results = jax.ShapeDtypeStruct((slots, voxels, channels), BF16)
    sums = (3, 16, 80, channels) if reduce_here else (3, 16, 9, 8, channels)
    outputs, grad, total = pl.pallas_call(
        functools.partial(kernel, n_gx, reduce_here),
        out_shape=(
            results,
            results,
            jax.ShapeDtypeStruct(sums, jnp.int16 if reduce_here else F32),
        ),
        in_specs=[smem, smem, any_space, any_space, any_space],
        out_specs=(any_space, any_space, vmem),
        scratch_shapes=[
            pltpu.VMEM((27, channels, channels), BF16),
            pltpu.VMEM((slots, voxels, channels), BF16),
            pltpu.VMEM((slots, voxels, channels), BF16),
            pltpu.VMEM((9 * slots + 1, 8, 64, channels), BF16),
            pltpu.VMEM((9 * slots + 1, 8, 64, channels), BF16),
            pltpu.VMEM((rows, 9 * channels), BF16),
            pltpu.VMEM((rows, 9 * channels), BF16),
            pltpu.VMEM((rows, 3 * channels), BF16),
            pltpu.VMEM((27 * channels, channels), BF16),
            pltpu.VMEM((3 * channels, 3 * channels), F32),
            pltpu.SMEM((slots, 27), jnp.int32),
            pltpu.VMEM((3, 16, 9, 8, channels), F32),
            pltpu.VMEM((3, 8, 9, 8, channels), F32),
            pltpu.VMEM((3, 4, 80, channels), jnp.int16),
            pltpu.VMEM((3, 4, 80, channels), jnp.int16),
            pltpu.VMEM((3, 3, 80, channels), jnp.int16),
            pltpu.VMEM((3, 3, 80, channels), jnp.int16),
            pltpu.SemaphoreType.DMA((5,)),
            pltpu.SemaphoreType.DMA((2, 5)),
            pltpu.SemaphoreType.DMA((2, 5)),
            pltpu.SemaphoreType.DMA((3, 10)),
            pltpu.SemaphoreType.DMA((3, 10)),
        ],
        compiler_params=pltpu.CompilerParams(
            collective_id=0, has_side_effects=True, vmem_limit_bytes=56 * 2**20
        ),
        cost_estimate=pl.CostEstimate(
            flops=6 * 27 * slots * voxels * channels * channels,
            bytes_accessed=8 * slots * voxels * channels,
            transcendentals=0,
        ),
    )(
        neighbours,
        counts,
        features.reshape(slots, 8, 64, channels),
        cotangent.reshape(slots, 8, 64, channels),
        weights,
    )
    if not reduce_here:
        total = lax.psum(total, ("gx", "gy"))
    outputs, grad, weight_grad = pl.pallas_call(
        functools.partial(finish, reduce_here),
        out_shape=(
            results,
            results,
            jax.ShapeDtypeStruct((3, 3, 3, 16, 8, channels), F32),
        ),
        in_specs=[vmem, any_space, any_space],
        out_specs=(any_space, any_space, vmem),
        scratch_shapes=[pltpu.SemaphoreType.DMA((2, slots))],
        compiler_params=pltpu.CompilerParams(vmem_limit_bytes=56 * 2**20),
    )(total, outputs, grad)
    return outputs, grad, weight_grad.reshape(27 * channels, channels)


def solution(mesh):
    return jax.shard_map(
        functools.partial(body, mesh.shape["gx"]),
        mesh=mesh,
        in_specs=(
            P(("parts", "gx", "gy"), None, None),
            P(("parts", "gx", "gy"), None, None),
            P(),
            P(("parts", "gx", "gy"), None),
            P(("parts", "gx", "gy")),
        ),
        out_specs=(
            P(("parts", "gx", "gy"), None, None),
            P(("parts", "gx", "gy"), None, None),
            P("parts", None),
        ),
        check_vma=False,
    )
```

```python
import functools

import jax
import jax.numpy as jnp
from jax import lax
from jax.experimental import pallas as pl
from jax.experimental.pallas import tpu as pltpu
from jax.sharding import PartitionSpec as P

MESH = pl.DeviceIdType.MESH
F32 = jnp.float32
BF16 = jnp.bfloat16


def encode(values):
    largest = jnp.max(jnp.abs(values), axis=0, keepdims=True)
    exponent = jnp.floor(jnp.log2(jnp.maximum(largest, 1e-30)) + 0.01) - 14.0
    scaled = jnp.floor(values * jnp.exp2(-exponent) + 0.5)
    both = jnp.concatenate([scaled, exponent], axis=0)
    return both.astype(jnp.int32).reshape(80, 128).astype(jnp.int16)


def decode(coded):
    both = coded.astype(jnp.int32).astype(F32).reshape(10, 8, 128)
    return both[:9] * jnp.exp2(both[9:])


def finish(
    coded,
    q_hbm,
    out_in,
    grad_in,
    out_hbm,
    grad_hbm,
    dw_hbm,
    q_ref,
    out_ref,
    grad_ref,
    dw_ref,
    in_sem,
    out_sem,
):
    arrays = [(q_hbm.at[t], q_ref.at[t], dw_ref.at[:, t], dw_hbm.at[:, t]) for t in range(3)]
    arrays += [(out_in, out_ref, out_ref, out_hbm), (grad_in, grad_ref, grad_ref, grad_hbm)]
    inward = [
        pltpu.make_async_copy(a[0], a[1], in_sem.at[k]) for k, a in enumerate(arrays)
    ]
    outward = [
        pltpu.make_async_copy(a[2], a[3], out_sem.at[k]) for k, a in enumerate(arrays)
    ]
    for copy in inward:
        copy.start()
    for t in range(3):
        inward[t].wait()

        def piece(share, carry):
            values = decode(q_ref[t, share]) if coded else q_ref[t, share]
            for a in range(3):
                for c in range(3):
                    dw_ref[a, t, c, share] = values[a * 3 + c]
            return carry

        lax.fori_loop(0, 16, piece, 0, unroll=4)
        outward[t].start()
    for k in (3, 4):
        inward[k].wait()
        outward[k].start()
    for copy in outward:
        copy.wait()


def kernel(
    n_gx,
    reduce_here,
    nb_ref,
    counts_ref,
    f_ref,
    g_ref,
    w_hbm,
    out_hbm,
    grad_hbm,
    dw_ref,
    w_ref,
    out_ref,
    grad_ref,
    table_f,
    table_g,
    x_f,
    x_g,
    m_cat,
    w_back,
    acc,
    idx,
    part,
    got_core,
    y_out,
    got_y,
    z_out,
    got_z,
    own_sem,
    halo_send,
    halo_recv,
    red_send,
    red_recv,
):
    slots = f_ref.shape[0]
    tables = (table_f, table_g)
    nothing = 9 * slots
    bits = slots.bit_length() - 1
    assert slots == 1 << bits
    rank = lax.axis_index("parts")
    gx = lax.axis_index("gx")
    gy = lax.axis_index("gy")
    other = 1 - gy
    up, down = lax.rem(gx + 1, n_gx), lax.rem(gx + n_gx - 1, n_gx)

    partners = [(up, gy), (down, gy), (gx, other), (up, other), (down, other)]
    if reduce_here:
        partners += [(lax.rem(gx + 2 * d, n_gx), gy) for d in (1, 2, 3)]
    barrier = pltpu.get_barrier_semaphore()
    for x, y in partners:
        pl.semaphore_signal(barrier, inc=1, device_id=(rank, x, y), device_id_type=MESH)

    own = [
        pltpu.make_async_copy(
            ref, tables[field].at[pl.ds(4 * slots, slots)], own_sem.at[field]
        )
        for field, ref in enumerate((f_ref, g_ref))
    ]
    for copy in own:
        copy.start()
    weights_in = pltpu.make_async_copy(w_hbm, w_ref, own_sem.at[2])
    weights_in.start()
    out_copy = pltpu.make_async_copy(out_ref, out_hbm, own_sem.at[3])
    grad_copy = pltpu.make_async_copy(grad_ref, grad_hbm, own_sem.at[4])
    pl.semaphore_wait(barrier, len(partners))

    line = pl.ds(pl.multiple_of(48 * other, 16), 16)
    has_up, has_down = gx < n_gx - 1, gx > 0

    def halo(field, ref, kind):
        table = tables[field]
        if kind == 0:
            source = ref.at[:, 7]
            target = table.at[pl.ds(1 * slots, slots), 7]
            device = (rank, up, gy)
        elif kind == 1:
            source = ref.at[:, 0]
            target = table.at[pl.ds(7 * slots, slots), 0]
            device = (rank, down, gy)
        elif kind == 2:
            source = ref.at[:, :, line]
            target = table.at[pl.ds((3 + 2 * gy) * slots, slots), :, line]
            device = (rank, gx, other)
        elif kind == 3:
            source = ref.at[:, 7, line]
            target = table.at[pl.ds(2 * gy * slots, slots), 7, line]
            device = (rank, up, other)
        else:
            source = ref.at[:, 0, line]
            target = table.at[pl.ds((6 + 2 * gy) * slots, slots), 0, line]
            device = (rank, down, other)
        return pltpu.make_async_remote_copy(
            src_ref=source,
            dst_ref=target,
            send_sem=halo_send.at[field, kind],
            recv_sem=halo_recv.at[field, kind],
            device_id=device,
            device_id_type=MESH,
        )

    copies = [[halo(field, ref, kind) for kind in range(5)] for field, ref in enumerate((f_ref, g_ref))]

    def start(field):
        @pl.when(has_up)
        def _():
            copies[field][0].start()
            copies[field][3].start()

        @pl.when(has_down)
        def _():
            copies[field][1].start()
            copies[field][4].start()

        copies[field][2].start()

    def arrived(field):
        @pl.when(has_down)
        def _():
            copies[field][0].wait_recv()
            copies[field][3].wait_recv()

        @pl.when(has_up)
        def _():
            copies[field][1].wait_recv()
            copies[field][4].wait_recv()

        copies[field][2].wait_recv()

    def sent(field):
        @pl.when(has_up)
        def _():
            copies[field][0].wait_send()
            copies[field][3].wait_send()

        @pl.when(has_down)
        def _():
            copies[field][1].wait_send()
            copies[field][4].wait_send()

        copies[field][2].wait_send()

    start(0)

    def fill(s, carry):
        for o in range(27):
            entry = nb_ref[s, o]
            safe = jnp.maximum(entry, 0)
            owner = safe >> bits
            relative = ((owner >> 1) - gx + 1) * 3 + ((owner & 1) - gy + 1)
            place = jnp.where(entry < 0, nothing, relative * slots + (safe & (slots - 1)))
            idx[s, o] = jnp.minimum(jnp.maximum(place, 0), nothing)
        return carry

    lax.fori_loop(0, slots, fill, 0)

    for field in range(2):
        tables[field][nothing] = jnp.zeros(table_f.shape[1:], BF16)

    for copy in own:
        copy.wait()

    def spread(s, carry):
        base = pl.multiple_of(s * 640, 128)
        value = table_g[4 * slots + s].reshape(512, 128)
        value = jnp.where(s < counts_ref[0], value.astype(F32), 0.0).astype(BF16)
        for a in range(3):
            columns = slice(a * 128, a * 128 + 128)
            if a > 0:
                m_cat[pl.ds(base, a * 64), columns] = jnp.zeros((a * 64, 128), BF16)
            if a < 2:
                m_cat[pl.ds(base + a * 64 + 512, 128 - a * 64), columns] = jnp.zeros(
                    (128 - a * 64, 128), BF16
                )
            m_cat[pl.ds(base + a * 64, 512), columns] = value
        return carry

    lax.fori_loop(0, slots, spread, 0)

    def turn(o, carry):
        rows = pl.ds(pl.multiple_of(o * 128, 128), 128)
        w_back[rows, :] = w_ref[26 - o].astype(F32).T.astype(BF16)
        return carry

    sub = lax.broadcasted_iota(jnp.int32, (10, 8, 128), 1)

    def build(table, x_ref):
        def plane(s, p, first, i):
            def gathered(z):
                low = table[idx[s, first + z], i, 48:64].astype(F32)[8:]
                mid = table[idx[s, first + 3 + z], i].astype(F32)
                high = table[idx[s, first + 6 + z], i, 0:16].astype(F32)[:8]
                return jnp.concatenate([low, mid, high], axis=0).reshape(10, 8, 128)

            below, here, above = gathered(0), gathered(1), gathered(2)
            lower = pltpu.roll(jnp.where(sub == 7, below, here), 1, 1)
            upper = pltpu.roll(jnp.where(sub == 0, above, here), 7, 1)
            rows = pl.ds(pl.multiple_of(s * 640 + p * 64, 64), 64)
            for c, value in enumerate((lower, here, upper)):
                for b in range(3):
                    o = b * 3 + c
                    x_ref[rows, o * 128 : o * 128 + 128] = (
                        value[b : b + 8].reshape(64, 128).astype(BF16)
                    )

        def brick(s, carry):
            plane(s, 0, 0, 7)
            plane(s, 9, 18, 0)

            def inner(i, carry):
                plane(s, i + 1, 9, i)
                return carry

            return lax.fori_loop(0, 8, inner, carry)

        lax.fori_loop(0, slots, brick, 0)

    def product(x_ref, weight, result, first, last):
        def brick(s, carry):
            total = jnp.zeros((512, 128), F32)
            for a in range(3):
                rows = pl.ds(pl.multiple_of(s * 640 + a * 64, 64), 512)
                total += jnp.dot(
                    x_ref[rows, :],
                    weight[a * 1152 : a * 1152 + 1152, :],
                    preferred_element_type=F32,
                )
            result[s] = jnp.where(s < counts_ref[0], total, 0.0).astype(BF16)
            return carry

        lax.fori_loop(first, last, brick, 0)

    def outer(t):
        acc[...] = jnp.zeros_like(acc)

        def brick(s, carry):
            rows = pl.ds(pl.multiple_of(s * 640, 128), 640)
            acc[...] += lax.dot_general(
                x_f[rows, t * 384 : t * 384 + 384],
                m_cat[rows, :],
                (((0,), (0,)), ((), ())),
                preferred_element_type=F32,
            )
            return carry

        lax.fori_loop(0, slots, brick, 0)
        target = part if reduce_here else dw_ref
        for a in range(3):
            for c in range(3):
                block = acc[c * 128 : c * 128 + 128, a * 128 : a * 128 + 128]
                target[t, :, a * 3 + c] = block.reshape(16, 8, 128)

    w_flat = w_ref.reshape(27 * 128, 128)

    weights_in.wait()
    lax.fori_loop(0, 27, turn, 0)
    arrived(0)
    start(1)
    build(table_f, x_f)
    if not reduce_here:
        for t in range(3):
            outer(t)
        arrived(1)
        build(table_g, x_g)
        product(x_f, w_flat, out_ref, 0, slots)
        out_copy.start()
        product(x_g, w_back, grad_ref, 0, slots)
        grad_copy.start()
        out_copy.wait()
        grad_copy.wait()
        sent(0)
        sent(1)
        return

    z, y = gx // 2, gx % 2
    half = 8 * gy
    quarter = half + 4 * y
    share = quarter + z
    side = (rank, z * 2 + 1 - y, gy)
    depth = [lax.rem(z + d, 4) for d in (1, 2, 3)]

    def send(t, k, source, target, device):
        return pltpu.make_async_remote_copy(
            src_ref=source,
            dst_ref=target,
            send_sem=red_send.at[t, k],
            recv_sem=red_recv.at[t, k],
            device_id=device,
            device_id_type=MESH,
        )

    core_step, y_step, z_step, z_back, y_back, core_back = [], [], [], [], [], []
    for t in range(3):
        core_step.append(
            send(t, 0, part.at[t, pl.ds(8 * other, 8)], got_core.at[t], (rank, gx, other))
        )
        y_step.append(send(t, 1, y_out.at[t], got_y.at[t], side))
        z_step.append(
            [
                send(t, 2 + d, z_out.at[t, d], got_z.at[t, d], (rank, depth[d] * 2 + y, gy))
                for d in range(3)
            ]
        )
        mine = dw_ref.at[t, share]
        z_back.append(
            [send(t, 5 + d, mine, mine, (rank, depth[d] * 2 + y, gy)) for d in range(3)]
        )
        mine = dw_ref.at[t, pl.ds(quarter, 4)]
        y_back.append(send(t, 8, mine, mine, side))
        mine = dw_ref.at[t, pl.ds(half, 8)]
        core_back.append(send(t, 9, mine, mine, (rank, gx, other)))

    def after_core(t):
        core_step[t].wait_recv()
        for j in range(4):
            place = 4 * (1 - y) + j
            y_out[t, j] = encode(part[t, half + place] + got_core[t, place])
        y_step[t].start()
        for j in range(4):
            place = 4 * y + j
            part[t, half + place] += got_core[t, place]

    def after_y(t):
        y_step[t].wait_recv()
        for d in range(3):
            z_out[t, d] = encode(part[t, quarter + depth[d]] + decode(got_y[t, depth[d]]))
        for copy in z_step[t]:
            copy.start()
        part[t, share] += decode(got_y[t, z])

    def after_z(t):
        for copy in z_step[t]:
            copy.wait_recv()
        dw_ref[t, share] = encode(
            (part[t, share] + decode(got_z[t, 0]))
            + (decode(got_z[t, 1]) + decode(got_z[t, 2]))
        )
        for copy in z_back[t]:
            copy.start()

    def after_z_back(t):
        for copy in z_back[t]:
            copy.wait_recv()
        y_back[t].start()

    def after_y_back(t):
        y_back[t].wait_recv()
        core_back[t].start()

    outer(0)
    core_step[0].start()
    outer(1)
    core_step[1].start()
    after_core(0)
    outer(2)
    core_step[2].start()
    after_core(1)
    arrived(1)
    after_core(2)
    build(table_g, x_g)
    after_y(0)
    mid = slots // 2
    product(x_f, w_flat, out_ref, 0, mid)
    after_y(1)
    product(x_f, w_flat, out_ref, mid, slots)
    out_copy.start()
    after_z(0)
    after_y(2)
    product(x_g, w_back, grad_ref, 0, mid)
    after_z(1)
    after_z_back(0)
    product(x_g, w_back, grad_ref, mid, slots)
    grad_copy.start()
    after_z(2)
    after_z_back(1)
    after_y_back(0)
    after_z_back(2)
    after_y_back(1)
    after_y_back(2)
    for t in range(3):
        core_back[t].wait_recv()
    out_copy.wait()
    grad_copy.wait()
    sent(0)
    sent(1)
    for t in range(3):
        for copy in [core_step[t], y_step[t], *z_step[t], *z_back[t], y_back[t], core_back[t]]:
            copy.wait_send()


def body(n_gx, features, cotangent, weights, neighbours, counts):
    slots, voxels, channels = features.shape
    reduce_here = n_gx == 8
    any_space = pl.BlockSpec(memory_space=pl.ANY)
    vmem = pl.BlockSpec(memory_space=pltpu.VMEM)
    smem = pl.BlockSpec(memory_space=pltpu.SMEM)
    rows = slots * 640
    results = jax.ShapeDtypeStruct((slots, voxels, channels), BF16)
    sums = (3, 16, 80, channels) if reduce_here else (3, 16, 9, 8, channels)
    outputs, grad, total = pl.pallas_call(
        functools.partial(kernel, n_gx, reduce_here),
        out_shape=(
            results,
            results,
            jax.ShapeDtypeStruct(sums, jnp.int16 if reduce_here else F32),
        ),
        in_specs=[smem, smem, any_space, any_space, any_space],
        out_specs=(any_space, any_space, vmem),
        scratch_shapes=[
            pltpu.VMEM((27, channels, channels), BF16),
            pltpu.VMEM((slots, voxels, channels), BF16),
            pltpu.VMEM((slots, voxels, channels), BF16),
            pltpu.VMEM((9 * slots + 1, 8, 64, channels), BF16),
            pltpu.VMEM((9 * slots + 1, 8, 64, channels), BF16),
            pltpu.VMEM((rows, 9 * channels), BF16),
            pltpu.VMEM((rows, 9 * channels), BF16),
            pltpu.VMEM((rows, 3 * channels), BF16),
            pltpu.VMEM((27 * channels, channels), BF16),
            pltpu.VMEM((3 * channels, 3 * channels), F32),
            pltpu.SMEM((slots, 27), jnp.int32),
            pltpu.VMEM((3, 16, 9, 8, channels), F32),
            pltpu.VMEM((3, 8, 9, 8, channels), F32),
            pltpu.VMEM((3, 4, 80, channels), jnp.int16),
            pltpu.VMEM((3, 4, 80, channels), jnp.int16),
            pltpu.VMEM((3, 3, 80, channels), jnp.int16),
            pltpu.VMEM((3, 3, 80, channels), jnp.int16),
            pltpu.SemaphoreType.DMA((5,)),
            pltpu.SemaphoreType.DMA((2, 5)),
            pltpu.SemaphoreType.DMA((2, 5)),
            pltpu.SemaphoreType.DMA((3, 10)),
            pltpu.SemaphoreType.DMA((3, 10)),
        ],
        compiler_params=pltpu.CompilerParams(
            collective_id=0, has_side_effects=True, vmem_limit_bytes=56 * 2**20
        ),
        cost_estimate=pl.CostEstimate(
            flops=6 * 27 * slots * voxels * channels * channels,
            bytes_accessed=8 * slots * voxels * channels,
            transcendentals=0,
        ),
    )(
        neighbours,
        counts,
        features.reshape(slots, 8, 64, channels),
        cotangent.reshape(slots, 8, 64, channels),
        weights,
    )
    if not reduce_here:
        total = lax.psum(total, ("gx", "gy"))
    outputs, grad, weight_grad = pl.pallas_call(
        functools.partial(finish, reduce_here),
        out_shape=(
            results,
            results,
            jax.ShapeDtypeStruct((3, 3, 3, 16, 8, channels), F32),
        ),
        in_specs=[any_space] * 3,
        out_specs=(any_space,) * 3,
        scratch_shapes=[
            pltpu.VMEM(total.shape, total.dtype),
            pltpu.VMEM((slots, voxels, channels), BF16),
            pltpu.VMEM((slots, voxels, channels), BF16),
            pltpu.VMEM((3, 3, 3, 16, 8, channels), F32),
            pltpu.SemaphoreType.DMA((5,)),
            pltpu.SemaphoreType.DMA((5,)),
        ],
        compiler_params=pltpu.CompilerParams(vmem_limit_bytes=56 * 2**20),
    )(total, outputs, grad)
    return outputs, grad, weight_grad.reshape(27 * channels, channels)


def solution(mesh):
    return jax.shard_map(
        functools.partial(body, mesh.shape["gx"]),
        mesh=mesh,
        in_specs=(
            P(("parts", "gx", "gy"), None, None),
            P(("parts", "gx", "gy"), None, None),
            P(),
            P(("parts", "gx", "gy"), None),
            P(("parts", "gx", "gy")),
        ),
        out_specs=(
            P(("parts", "gx", "gy"), None, None),
            P(("parts", "gx", "gy"), None, None),
            P("parts", None),
        ),
        check_vma=False,
    )
```

```python
import functools

import jax
import jax.numpy as jnp
from jax import lax
from jax.experimental import pallas as pl
from jax.experimental.pallas import tpu as pltpu
from jax.sharding import PartitionSpec as P

MESH = pl.DeviceIdType.MESH
F32 = jnp.float32
BF16 = jnp.bfloat16


def encode(values):
    largest = jnp.max(jnp.abs(values), axis=0, keepdims=True)
    exponent = jnp.floor(jnp.log2(jnp.maximum(largest, 1e-30)) + 0.01) - 14.0
    scaled = jnp.floor(values * jnp.exp2(-exponent) + 0.5)
    both = jnp.concatenate([scaled, exponent], axis=0)
    return both.astype(jnp.int32).reshape(80, 128).astype(jnp.int16)


def decode(coded):
    both = coded.astype(jnp.int32).astype(F32).reshape(10, 8, 128)
    return both[:9] * jnp.exp2(both[9:])


def finish(
    coded,
    q_hbm,
    out_in,
    grad_in,
    out_hbm,
    grad_hbm,
    dw_hbm,
    q_ref,
    out_ref,
    grad_ref,
    dw_ref,
    in_sem,
    out_sem,
):
    arrays = [(q_hbm.at[t], q_ref.at[t], dw_ref.at[:, t], dw_hbm.at[:, t]) for t in range(3)]
    arrays += [(out_in, out_ref, out_ref, out_hbm), (grad_in, grad_ref, grad_ref, grad_hbm)]
    inward = [
        pltpu.make_async_copy(a[0], a[1], in_sem.at[k]) for k, a in enumerate(arrays)
    ]
    outward = [
        pltpu.make_async_copy(a[2], a[3], out_sem.at[k]) for k, a in enumerate(arrays)
    ]
    for copy in inward:
        copy.start()
    for t in range(3):
        inward[t].wait()

        def piece(share, carry):
            values = decode(q_ref[t, share]) if coded else q_ref[t, share]
            for a in range(3):
                for c in range(3):
                    dw_ref[a, t, c, share] = values[a * 3 + c]
            return carry

        lax.fori_loop(0, 16, piece, 0, unroll=4)
        outward[t].start()
    for k in (3, 4):
        inward[k].wait()
        outward[k].start()
    for copy in outward:
        copy.wait()


def kernel(
    n_gx,
    reduce_here,
    nb_ref,
    counts_ref,
    f_ref,
    g_ref,
    w_hbm,
    out_hbm,
    grad_hbm,
    dw_ref,
    w_ref,
    out_ref,
    grad_ref,
    table_f,
    table_g,
    x_f,
    x_g,
    m_cat,
    w_back,
    acc,
    idx,
    part,
    got_core,
    y_out,
    got_y,
    z_out,
    got_z,
    own_sem,
    halo_send,
    halo_recv,
    red_send,
    red_recv,
):
    slots = f_ref.shape[0]
    tables = (table_f, table_g)
    nothing = 9 * slots
    bits = slots.bit_length() - 1
    assert slots == 1 << bits
    rank = lax.axis_index("parts")
    gx = lax.axis_index("gx")
    gy = lax.axis_index("gy")
    other = 1 - gy
    up, down = lax.rem(gx + 1, n_gx), lax.rem(gx + n_gx - 1, n_gx)

    partners = [(up, gy), (down, gy), (gx, other), (up, other), (down, other)]
    if reduce_here:
        partners += [(lax.rem(gx + 2 * d, n_gx), gy) for d in (1, 2, 3)]
    barrier = pltpu.get_barrier_semaphore()
    for x, y in partners:
        pl.semaphore_signal(barrier, inc=1, device_id=(rank, x, y), device_id_type=MESH)

    own = [
        pltpu.make_async_copy(
            ref, tables[field].at[pl.ds(4 * slots, slots)], own_sem.at[field]
        )
        for field, ref in enumerate((f_ref, g_ref))
    ]
    for copy in own:
        copy.start()
    weights_in = pltpu.make_async_copy(w_hbm, w_ref, own_sem.at[2])
    weights_in.start()
    out_copy = pltpu.make_async_copy(out_ref, out_hbm, own_sem.at[3])
    grad_copy = pltpu.make_async_copy(grad_ref, grad_hbm, own_sem.at[4])
    pl.semaphore_wait(barrier, len(partners))

    line = pl.ds(pl.multiple_of(48 * other, 16), 16)
    has_up, has_down = gx < n_gx - 1, gx > 0

    def halo(field, ref, kind):
        table = tables[field]
        if kind == 0:
            source = ref.at[:, 7]
            target = table.at[pl.ds(1 * slots, slots), 7]
            device = (rank, up, gy)
        elif kind == 1:
            source = ref.at[:, 0]
            target = table.at[pl.ds(7 * slots, slots), 0]
            device = (rank, down, gy)
        elif kind == 2:
            source = ref.at[:, :, line]
            target = table.at[pl.ds((3 + 2 * gy) * slots, slots), :, line]
            device = (rank, gx, other)
        elif kind == 3:
            source = ref.at[:, 7, line]
            target = table.at[pl.ds(2 * gy * slots, slots), 7, line]
            device = (rank, up, other)
        else:
            source = ref.at[:, 0, line]
            target = table.at[pl.ds((6 + 2 * gy) * slots, slots), 0, line]
            device = (rank, down, other)
        return pltpu.make_async_remote_copy(
            src_ref=source,
            dst_ref=target,
            send_sem=halo_send.at[field, kind],
            recv_sem=halo_recv.at[field, kind],
            device_id=device,
            device_id_type=MESH,
        )

    copies = [[halo(field, ref, kind) for kind in range(5)] for field, ref in enumerate((f_ref, g_ref))]

    def start(field):
        @pl.when(has_up)
        def _():
            copies[field][0].start()
            copies[field][3].start()

        @pl.when(has_down)
        def _():
            copies[field][1].start()
            copies[field][4].start()

        copies[field][2].start()

    def arrived(field):
        @pl.when(has_down)
        def _():
            copies[field][0].wait_recv()
            copies[field][3].wait_recv()

        @pl.when(has_up)
        def _():
            copies[field][1].wait_recv()
            copies[field][4].wait_recv()

        copies[field][2].wait_recv()

    def sent(field):
        @pl.when(has_up)
        def _():
            copies[field][0].wait_send()
            copies[field][3].wait_send()

        @pl.when(has_down)
        def _():
            copies[field][1].wait_send()
            copies[field][4].wait_send()

        copies[field][2].wait_send()

    start(0)

    def fill(s, carry):
        for o in range(27):
            entry = nb_ref[s, o]
            safe = jnp.maximum(entry, 0)
            owner = safe >> bits
            relative = ((owner >> 1) - gx + 1) * 3 + ((owner & 1) - gy + 1)
            place = jnp.where(entry < 0, nothing, relative * slots + (safe & (slots - 1)))
            idx[s, o] = jnp.minimum(jnp.maximum(place, 0), nothing)
        return carry

    lax.fori_loop(0, slots, fill, 0)

    for field in range(2):
        tables[field][nothing] = jnp.zeros(table_f.shape[1:], BF16)

    for copy in own:
        copy.wait()

    def spread(s, carry):
        base = pl.multiple_of(s * 640, 128)
        value = table_g[4 * slots + s].reshape(512, 128)
        value = jnp.where(s < counts_ref[0], value.astype(F32), 0.0).astype(BF16)
        for a in range(3):
            columns = slice(a * 128, a * 128 + 128)
            if a > 0:
                m_cat[pl.ds(base, a * 64), columns] = jnp.zeros((a * 64, 128), BF16)
            if a < 2:
                m_cat[pl.ds(base + a * 64 + 512, 128 - a * 64), columns] = jnp.zeros(
                    (128 - a * 64, 128), BF16
                )
            m_cat[pl.ds(base + a * 64, 512), columns] = value
        return carry

    lax.fori_loop(0, slots, spread, 0)

    def turn(o, carry):
        rows = pl.ds(pl.multiple_of(o * 128, 128), 128)
        w_back[rows, :] = w_ref[26 - o].astype(F32).T.astype(BF16)
        return carry

    sub = lax.broadcasted_iota(jnp.int32, (10, 8, 128), 1)

    def build(table, x_ref):
        def plane(s, p, first, i):
            def gathered(z):
                low = table[idx[s, first + z], i, 48:64].astype(F32)[8:]
                mid = table[idx[s, first + 3 + z], i].astype(F32)
                high = table[idx[s, first + 6 + z], i, 0:16].astype(F32)[:8]
                return jnp.concatenate([low, mid, high], axis=0).reshape(10, 8, 128)

            below, here, above = gathered(0), gathered(1), gathered(2)
            lower = pltpu.roll(jnp.where(sub == 7, below, here), 1, 1)
            upper = pltpu.roll(jnp.where(sub == 0, above, here), 7, 1)
            rows = pl.ds(pl.multiple_of(s * 640 + p * 64, 64), 64)
            for c, value in enumerate((lower, here, upper)):
                for b in range(3):
                    o = b * 3 + c
                    x_ref[rows, o * 128 : o * 128 + 128] = (
                        value[b : b + 8].reshape(64, 128).astype(BF16)
                    )

        def brick(s, carry):
            plane(s, 0, 0, 7)
            plane(s, 9, 18, 0)

            def inner(i, carry):
                plane(s, i + 1, 9, i)
                return carry

            return lax.fori_loop(0, 8, inner, carry)

        lax.fori_loop(0, slots, brick, 0)

    def product(x_ref, weight, result, first, last):
        def brick(s, carry):
            total = jnp.zeros((512, 128), F32)
            for a in range(3):
                rows = pl.ds(pl.multiple_of(s * 640 + a * 64, 64), 512)
                total += jnp.dot(
                    x_ref[rows, :],
                    weight[a * 1152 : a * 1152 + 1152, :],
                    preferred_element_type=F32,
                )
            result[s] = jnp.where(s < counts_ref[0], total, 0.0).astype(BF16)
            return carry

        lax.fori_loop(first, last, brick, 0)

    def outer(t):
        acc[...] = lax.dot_general(
            x_f[:, t * 384 : t * 384 + 384],
            m_cat[...],
            (((0,), (0,)), ((), ())),
            preferred_element_type=F32,
        )
        target = part if reduce_here else dw_ref
        for a in range(3):
            for c in range(3):
                block = acc[c * 128 : c * 128 + 128, a * 128 : a * 128 + 128]
                target[t, :, a * 3 + c] = block.reshape(16, 8, 128)

    w_flat = w_ref.reshape(27 * 128, 128)

    weights_in.wait()
    lax.fori_loop(0, 27, turn, 0)
    arrived(0)
    start(1)
    build(table_f, x_f)
    if not reduce_here:
        for t in range(3):
            outer(t)
        arrived(1)
        build(table_g, x_g)
        product(x_f, w_flat, out_ref, 0, slots)
        out_copy.start()
        product(x_g, w_back, grad_ref, 0, slots)
        grad_copy.start()
        out_copy.wait()
        grad_copy.wait()
        sent(0)
        sent(1)
        return

    z, y = gx // 2, gx % 2
    half = 8 * gy
    quarter = half + 4 * y
    share = quarter + z
    side = (rank, z * 2 + 1 - y, gy)
    depth = [lax.rem(z + d, 4) for d in (1, 2, 3)]

    def send(t, k, source, target, device):
        return pltpu.make_async_remote_copy(
            src_ref=source,
            dst_ref=target,
            send_sem=red_send.at[t, k],
            recv_sem=red_recv.at[t, k],
            device_id=device,
            device_id_type=MESH,
        )

    core_step, y_step, z_step, z_back, y_back, core_back = [], [], [], [], [], []
    for t in range(3):
        core_step.append(
            send(t, 0, part.at[t, pl.ds(8 * other, 8)], got_core.at[t], (rank, gx, other))
        )
        y_step.append(send(t, 1, y_out.at[t], got_y.at[t], side))
        z_step.append(
            [
                send(t, 2 + d, z_out.at[t, d], got_z.at[t, d], (rank, depth[d] * 2 + y, gy))
                for d in range(3)
            ]
        )
        mine = dw_ref.at[t, share]
        z_back.append(
            [send(t, 5 + d, mine, mine, (rank, depth[d] * 2 + y, gy)) for d in range(3)]
        )
        mine = dw_ref.at[t, pl.ds(quarter, 4)]
        y_back.append(send(t, 8, mine, mine, side))
        mine = dw_ref.at[t, pl.ds(half, 8)]
        core_back.append(send(t, 9, mine, mine, (rank, gx, other)))

    def after_core(t):
        core_step[t].wait_recv()
        for j in range(4):
            place = 4 * (1 - y) + j
            y_out[t, j] = encode(part[t, half + place] + got_core[t, place])
        y_step[t].start()
        for j in range(4):
            place = 4 * y + j
            part[t, half + place] += got_core[t, place]

    def after_y(t):
        y_step[t].wait_recv()
        for d in range(3):
            z_out[t, d] = encode(part[t, quarter + depth[d]] + decode(got_y[t, depth[d]]))
        for copy in z_step[t]:
            copy.start()
        part[t, share] += decode(got_y[t, z])

    def after_z(t):
        for copy in z_step[t]:
            copy.wait_recv()
        dw_ref[t, share] = encode(
            (part[t, share] + decode(got_z[t, 0]))
            + (decode(got_z[t, 1]) + decode(got_z[t, 2]))
        )
        for copy in z_back[t]:
            copy.start()

    def after_z_back(t):
        for copy in z_back[t]:
            copy.wait_recv()
        y_back[t].start()

    def after_y_back(t):
        y_back[t].wait_recv()
        core_back[t].start()

    outer(0)
    core_step[0].start()
    outer(1)
    core_step[1].start()
    after_core(0)
    outer(2)
    core_step[2].start()
    after_core(1)
    arrived(1)
    after_core(2)
    build(table_g, x_g)
    after_y(0)
    mid = slots // 2
    product(x_f, w_flat, out_ref, 0, mid)
    after_y(1)
    product(x_f, w_flat, out_ref, mid, slots)
    out_copy.start()
    after_z(0)
    after_y(2)
    product(x_g, w_back, grad_ref, 0, mid)
    after_z(1)
    after_z_back(0)
    product(x_g, w_back, grad_ref, mid, slots)
    grad_copy.start()
    after_z(2)
    after_z_back(1)
    after_y_back(0)
    after_z_back(2)
    after_y_back(1)
    after_y_back(2)
    for t in range(3):
        core_back[t].wait_recv()
    out_copy.wait()
    grad_copy.wait()
    sent(0)
    sent(1)
    for t in range(3):
        for copy in [core_step[t], y_step[t], *z_step[t], *z_back[t], y_back[t], core_back[t]]:
            copy.wait_send()


def body(n_gx, features, cotangent, weights, neighbours, counts):
    slots, voxels, channels = features.shape
    reduce_here = n_gx == 8
    any_space = pl.BlockSpec(memory_space=pl.ANY)
    vmem = pl.BlockSpec(memory_space=pltpu.VMEM)
    smem = pl.BlockSpec(memory_space=pltpu.SMEM)
    rows = slots * 640
    results = jax.ShapeDtypeStruct((slots, voxels, channels), BF16)
    sums = (3, 16, 80, channels) if reduce_here else (3, 16, 9, 8, channels)
    outputs, grad, total = pl.pallas_call(
        functools.partial(kernel, n_gx, reduce_here),
        out_shape=(
            results,
            results,
            jax.ShapeDtypeStruct(sums, jnp.int16 if reduce_here else F32),
        ),
        in_specs=[smem, smem, any_space, any_space, any_space],
        out_specs=(any_space, any_space, vmem),
        scratch_shapes=[
            pltpu.VMEM((27, channels, channels), BF16),
            pltpu.VMEM((slots, voxels, channels), BF16),
            pltpu.VMEM((slots, voxels, channels), BF16),
            pltpu.VMEM((9 * slots + 1, 8, 64, channels), BF16),
            pltpu.VMEM((9 * slots + 1, 8, 64, channels), BF16),
            pltpu.VMEM((rows, 9 * channels), BF16),
            pltpu.VMEM((rows, 9 * channels), BF16),
            pltpu.VMEM((rows, 3 * channels), BF16),
            pltpu.VMEM((27 * channels, channels), BF16),
            pltpu.VMEM((3 * channels, 3 * channels), F32),
            pltpu.SMEM((slots, 27), jnp.int32),
            pltpu.VMEM((3, 16, 9, 8, channels), F32),
            pltpu.VMEM((3, 8, 9, 8, channels), F32),
            pltpu.VMEM((3, 4, 80, channels), jnp.int16),
            pltpu.VMEM((3, 4, 80, channels), jnp.int16),
            pltpu.VMEM((3, 3, 80, channels), jnp.int16),
            pltpu.VMEM((3, 3, 80, channels), jnp.int16),
            pltpu.SemaphoreType.DMA((5,)),
            pltpu.SemaphoreType.DMA((2, 5)),
            pltpu.SemaphoreType.DMA((2, 5)),
            pltpu.SemaphoreType.DMA((3, 10)),
            pltpu.SemaphoreType.DMA((3, 10)),
        ],
        compiler_params=pltpu.CompilerParams(
            collective_id=0, has_side_effects=True, vmem_limit_bytes=56 * 2**20
        ),
        cost_estimate=pl.CostEstimate(
            flops=6 * 27 * slots * voxels * channels * channels,
            bytes_accessed=8 * slots * voxels * channels,
            transcendentals=0,
        ),
    )(
        neighbours,
        counts,
        features.reshape(slots, 8, 64, channels),
        cotangent.reshape(slots, 8, 64, channels),
        weights,
    )
    if not reduce_here:
        total = lax.psum(total, ("gx", "gy"))
    outputs, grad, weight_grad = pl.pallas_call(
        functools.partial(finish, reduce_here),
        out_shape=(
            results,
            results,
            jax.ShapeDtypeStruct((3, 3, 3, 16, 8, channels), F32),
        ),
        in_specs=[any_space] * 3,
        out_specs=(any_space,) * 3,
        scratch_shapes=[
            pltpu.VMEM(total.shape, total.dtype),
            pltpu.VMEM((slots, voxels, channels), BF16),
            pltpu.VMEM((slots, voxels, channels), BF16),
            pltpu.VMEM((3, 3, 3, 16, 8, channels), F32),
            pltpu.SemaphoreType.DMA((5,)),
            pltpu.SemaphoreType.DMA((5,)),
        ],
        compiler_params=pltpu.CompilerParams(vmem_limit_bytes=56 * 2**20),
    )(total, outputs, grad)
    return outputs, grad, weight_grad.reshape(27 * channels, channels)


def solution(mesh):
    return jax.shard_map(
        functools.partial(body, mesh.shape["gx"]),
        mesh=mesh,
        in_specs=(
            P(("parts", "gx", "gy"), None, None),
            P(("parts", "gx", "gy"), None, None),
            P(),
            P(("parts", "gx", "gy"), None),
            P(("parts", "gx", "gy")),
        ),
        out_specs=(
            P(("parts", "gx", "gy"), None, None),
            P(("parts", "gx", "gy"), None, None),
            P("parts", None),
        ),
        check_vma=False,
    )
```
